1024 devices in a mesh: row: 32 (over x, z_hi, core), col: 32 (over y, z_lo).
Axes of the slice: x: 4, y: 4, z: 32 (z_hi: 4, z_lo: 8; z = z_hi * 8 + z_lo), core: 2. Of those that a mesh axis runs over, the one named last changes fastest.
Arguments:
- left_blocks: bfloat16 [32, 32, 24, 128, 128], P('row', 'col'), may hold values from -0.5 to 0.5
- left_where: int32 [32, 32, 24], P('row', 'col'), may hold values from 0 to 48, as said below
- right_blocks: bfloat16 [32, 32, 32, 128, 128], P('row', 'col'), may hold values from -6 to 6
- right_where: int32 [32, 32, 32], P('row', 'col'), may hold values from 0 to 64, as said below
- keep_where: int32 [32, 32, 24], P('row', 'col'), may hold values from 0 to 47, as said below
Outputs:
- result_blocks: float32 [32, 32, 24, 128, 128], P('row', 'col')
The draws below stay inside these ranges and needn't reach their ends.
Inputs may be any that keep to these rules, and one draw needn't show every extreme that they name: `left_where`: in each grid position the live slots name distinct block positions; empty slots hold 48; at least 12 slots of every panel are live, and some panel has all of them live. `right_where`: in each grid position the live slots name distinct block positions; empty slots hold 64; at least 16 slots of every panel are live, and some panel has all of them live. `keep_where`: distinct within each grid position.
All inputs are finite; a program needn't handle non-finite values.
Results may differ from the reference program's by a relative error of at most 0.0003.
Values may be sent and summed in bfloat16 or wider, within the bound.
No kernel may reach another device: no remote copies, remote signals or barrier semaphores. Data moves between devices by JAX's collectives and lax.ppermute only.
A program may use at most 32 MiB of HBM per device.

```python
import jax
import jax.numpy as jnp
from jax import lax

BLK = 128
MB = 6
KW = 8
NB = 8
SLOTS_A = 24
SLOTS_B = 32
SLOTS_C = 24
GR = 32
GC = 32


def slot_lists(key, places, slots):
    count = GR * GC
    full_index = jax.random.randint(jax.random.fold_in(key, 5), (), 0, count)

    def one_panel(sub, index):
        first_key, second_key, third_key = jax.random.split(sub, 3)
        order = jax.random.permutation(first_key, places)[:slots]
        live_count = jax.random.randint(second_key, (), slots // 2, slots + 1)
        live_count = jnp.where(index == full_index, slots, live_count)
        shuffle = jax.random.permutation(third_key, slots)
        return jnp.where(shuffle < live_count, order, places).astype(jnp.int32)
    subkeys = jax.random.split(jax.random.fold_in(key, 9), count)
    lists = jax.vmap(one_panel)(subkeys, jnp.arange(count, dtype=jnp.int32))
    return lists.reshape(GR, GC, slots)


def draw_left_where(key, part):
    key = jax.random.fold_in(key, 11)
    return slot_lists(key, MB * KW, SLOTS_A)


def draw_right_where(key, part):
    key = jax.random.fold_in(key, 12)
    return slot_lists(key, KW * NB, SLOTS_B)


def draw_keep_where(key, part):
    key = jax.random.fold_in(key, 13)
    count = GR * GC

    def one_panel(sub):
        return jax.random.permutation(sub, MB * NB)[:SLOTS_C].astype(jnp.int32)
    lists = jax.vmap(one_panel)(jax.random.split(key, count))
    return lists.reshape(GR, GC, SLOTS_C)


def block_scale(rng, dims, cuts, least, top_value):
    gain, own = 1.0, jax.random.fold_in(rng, 6)
    for dim, blocks in cuts:
        draws = jnp.exp(jax.random.uniform(jax.random.fold_in(own, dim), (blocks,), jnp.float32, least / len(cuts), top_value / len(cuts)))
        gain = gain * jnp.repeat(draws, dims[dim] // blocks).reshape([-1 if axis == dim else 1 for axis in range(len(dims))])
    return gain


def gaussian(rng, dims, spread, bound, cuts=(), kind=jnp.bfloat16):
    drawn = spread * jax.random.normal(rng, dims, jnp.float32)
    if cuts:
        drawn = drawn * block_scale(rng, dims, cuts, -0.22, 0.18)
    return jnp.clip(drawn, -bound, bound).astype(kind)


def setup_inputs(seed: int = 0) -> dict:
    keys = jax.random.split(jax.random.key(seed), 6)
    left_blocks = gaussian(keys[0], (GR, GC, SLOTS_A, BLK, BLK), BLK ** -0.5, 0.5, ((0, 32), (1, 32)))
    left_where = draw_left_where(jax.random.fold_in(keys[5], 71), 0)
    right_blocks = gaussian(keys[2], (GR, GC, SLOTS_B, BLK, BLK), 1.0, 6.0, ((0, 32), (1, 32)))
    right_where = draw_right_where(jax.random.fold_in(keys[5], 71), 0)
    keep_where = draw_keep_where(jax.random.fold_in(keys[5], 71), 0)
    return dict(left_blocks=left_blocks, left_where=left_where, right_blocks=right_blocks, right_where=right_where, keep_where=keep_where)


def pack_panel(blocks, where, rows, cols):
    empty = jnp.zeros((rows * cols, BLK, BLK), jnp.float32)
    filled = empty.at[where].set(blocks.astype(jnp.float32), mode="drop")
    return filled.reshape(rows, cols, BLK, BLK)


def multiply(left, right):
    return jnp.einsum("ikab,kjbc->ijac", left, right, precision=lax.Precision.HIGHEST)


def device_product(pieces):
    left_mine, left_mine_where, right_mine, right_mine_where, left_next, left_next_where, right_next, right_next_where, kept = pieces
    first = multiply(pack_panel(left_mine, left_mine_where, MB, KW), pack_panel(right_mine, right_mine_where, KW, NB))
    second = multiply(pack_panel(left_next, left_next_where, MB, KW), pack_panel(right_next, right_next_where, KW, NB))
    product = (first + second).reshape(MB * NB, BLK, BLK)
    return jnp.take(product, kept, axis=0)


def reference(left_blocks, left_where, right_blocks, right_where, keep_where):
    count = GR * GC
    left_next = jnp.roll(left_blocks, -1, axis=1)
    left_next_where = jnp.roll(left_where, -1, axis=1)
    right_next = jnp.roll(right_blocks, -1, axis=0)
    right_next_where = jnp.roll(right_where, -1, axis=0)
    pieces = (
        left_blocks.reshape(count, SLOTS_A, BLK, BLK),
        left_where.reshape(count, SLOTS_A),
        right_blocks.reshape(count, SLOTS_B, BLK, BLK),
        right_where.reshape(count, SLOTS_B),
        left_next.reshape(count, SLOTS_A, BLK, BLK),
        left_next_where.reshape(count, SLOTS_A),
        right_next.reshape(count, SLOTS_B, BLK, BLK),
        right_next_where.reshape(count, SLOTS_B),
        keep_where.reshape(count, SLOTS_C),
    )
    result = lax.map(device_product, pieces)
    return result.reshape(GR, GC, SLOTS_C, BLK, BLK)
```

```python
import jax
import jax.numpy as jnp
from jax import lax
from jax.experimental import pallas as pl
from jax.experimental.pallas import tpu as pltpu
from jax.sharding import PartitionSpec as P

BLK = 128
MB = 6
KW = 8
NB = 8
SLOTS_A = 24
SLOTS_B = 32
SLOTS_C = 24
STEP = 2
AXES = ("row", "col")
VMEM_LIMIT = 40 * 1024 * 1024

SMEM_SPEC = pl.BlockSpec(memory_space=pltpu.SMEM)
VMEM_SPEC = pl.BlockSpec(memory_space=pltpu.VMEM)
ANY_SPEC = pl.BlockSpec(memory_space=pl.ANY)


def plan_kernel(across, mine, theirs, blocks, meta, packed, left_mask, keep_mask, sems):
    sends = across[0] == 0

    def right_at(s):
        return jnp.where(sends, mine[s], theirs[s])

    def keep_at(u):
        return jnp.where(sends, theirs[SLOTS_B + u], mine[SLOTS_B + u])

    def left_at(s):
        at = SLOTS_B + SLOTS_C + s
        return jnp.where(sends, theirs[at], mine[at])

    for k in range(KW + 1):
        left_mask[k] = 0
    for j in range(NB):
        keep_mask[j] = 0
    for s in range(SLOTS_A):
        w = left_at(s)
        bit = jnp.where(w < MB * KW, lax.shift_left(jnp.int32(1), w >> 3), 0)
        left_mask[w & 7] = left_mask[w & 7] | bit
    for u in range(SLOTS_C):
        w = keep_at(u)
        keep_mask[w & 7] = keep_mask[w & 7] | lax.shift_left(jnp.int32(1), w >> 3)

    def copy(s, n):
        return pltpu.make_async_copy(blocks.at[s], packed.at[n], sems.at[n])

    n = jnp.int32(0)
    for s in range(SLOTS_B):
        w = right_at(s)
        need = (left_mask[w >> 3] & keep_mask[w & 7]) != 0

        @pl.when(need)
        def _(s=s, n=n, w=w):
            meta[1 + n] = w

            @pl.when(sends)
            def _():
                copy(s, n).start()

        n = n + need.astype(jnp.int32)
    meta[0] = n

    @pl.when(sends)
    def _():
        @pl.loop(0, n)
        def _(t):
            copy(0, t).wait()


def fill_right(panel, where_at, blocks, count):
    @pl.loop(0, count)
    def _(s):
        w = where_at(s)
        at = pl.multiple_of((w >> 3) * BLK, BLK)
        panel[w & 7, pl.ds(at, BLK), :] = blocks[s]


def fill_left(panel, where, blocks):
    panel[...] = jnp.zeros_like(panel)
    for s in range(SLOTS_A):
        w = where[s]
        at = pl.multiple_of((w & 7) * BLK, BLK)
        panel[w >> 3, :, pl.ds(at, BLK)] = blocks[s]


def block_product(left, right, w):
    return jnp.dot(
        left[w >> 3], right[w & 7, : KW * BLK, :], preferred_element_type=jnp.float32
    )


def own_kernel(lw, rw, kw, left_blocks, right_blocks, total, left, right):
    fill_left(left, lw, left_blocks)
    right[...] = jnp.zeros_like(right)
    fill_right(right, lambda s: rw[s], right_blocks, SLOTS_B)
    for u in range(SLOTS_C):
        total[u] = block_product(left, right, kw[u])


def right_kernel(across, meta, rw, arrived, beside, right):
    right[...] = jnp.zeros_like(right)

    @pl.when(across[0] == 0)
    def _():
        fill_right(right, lambda s: rw[s], beside, SLOTS_B)

    @pl.when(across[0] != 0)
    def _():
        fill_right(right, lambda s: meta[1 + s], arrived, meta[0])


def last_kernel(lw, kw, left_blocks, right, total, out, left):
    fill_left(left, lw, left_blocks)
    for u in range(SLOTS_C):
        out[u] = total[u] + block_product(left, right, kw[u])


def call(kernel, out_shape, in_specs, out_specs, scratch, flops, moved):
    return pl.pallas_call(
        kernel,
        out_shape=out_shape,
        in_specs=in_specs,
        out_specs=out_specs,
        scratch_shapes=scratch,
        compiler_params=pltpu.CompilerParams(vmem_limit_bytes=VMEM_LIMIT),
        cost_estimate=pl.CostEstimate(flops=flops, bytes_accessed=moved, transcendentals=0),
    )


LEFT_PANEL = (MB + 1, BLK, KW * BLK)
RIGHT_PANEL = (NB, (KW + 1) * BLK, BLK)
FLOPS = 2 * SLOTS_C * KW * BLK**3


def on_device(left_blocks, left_where, right_blocks, right_where, keep_where):
    lb, lw = left_blocks[0, 0], left_where[0, 0]
    rb, rw = right_blocks[0, 0], right_where[0, 0]
    kw = keep_where[0, 0]
    rows, cols = lax.axis_size("row"), lax.axis_size("col")

    def at(p, q):
        return (p % rows) * cols + q % cols

    grid = [(p, q) for p in range(rows) for q in range(cols)]
    across = [(at(p + 1, q), at(p, q)) for p, q in grid if p % 2 == 1]
    beside = [(at(p + 1, q), at(p, q)) for p, q in grid if p % 2 == 0]
    swap = across + [(b, a) for a, b in across]
    left_on = [(at(p, q + 1), at(p, q)) for p, q in grid]
    side = (lax.axis_index("row") % 2).astype(jnp.int32)[None]

    lw2 = lax.ppermute(lw, AXES, left_on)
    mine = jnp.concatenate([rw, kw, lw2])
    theirs = lax.ppermute(mine, AXES, swap)
    rw2 = lax.ppermute(rw, AXES, beside)
    beside_blocks = lax.ppermute(rb, AXES, beside)
    lb2 = lax.ppermute(lb, AXES, left_on)

    meta, packed = call(
        plan_kernel,
        (
            jax.ShapeDtypeStruct((SLOTS_B + 1,), jnp.int32),
            jax.ShapeDtypeStruct(rb.shape, rb.dtype),
        ),
        [SMEM_SPEC, SMEM_SPEC, SMEM_SPEC, ANY_SPEC],
        (SMEM_SPEC, VMEM_SPEC),
        [
            pltpu.SMEM((KW + 1,), jnp.int32),
            pltpu.SMEM((NB,), jnp.int32),
            pltpu.SemaphoreType.DMA((SLOTS_B,)),
        ],
        0,
        2 * rb.size,
    )(side, mine, theirs, rb)

    def branch(size):
        def body(packed, meta, rw2, beside_blocks, lb, lw, rb, rw, kw):
            arrived = lax.ppermute(packed[:size], AXES, across)
            total = call(
                own_kernel,
                jax.ShapeDtypeStruct((SLOTS_C, BLK, BLK), jnp.float32),
                [SMEM_SPEC] * 3 + [VMEM_SPEC] * 2,
                VMEM_SPEC,
                [pltpu.VMEM(LEFT_PANEL, lb.dtype), pltpu.VMEM(RIGHT_PANEL, rb.dtype)],
                FLOPS,
                4 * SLOTS_C * BLK * BLK,
            )(lw, rw, kw, lb, rb)
            right = call(
                right_kernel,
                jax.ShapeDtypeStruct(RIGHT_PANEL, rb.dtype),
                [SMEM_SPEC] * 3 + [VMEM_SPEC] * 2,
                VMEM_SPEC,
                [],
                0,
                2 * rb.size,
            )(side, meta, rw2, arrived, beside_blocks)
            return total, right

        return body

    sizes = range(STEP, SLOTS_B + 1, STEP)
    pick = jnp.maximum((meta[0] + (STEP - 1)) // STEP, 1) - 1
    total, right = lax.switch(
        pick,
        [branch(size) for size in sizes],
        packed, meta, rw2, beside_blocks, lb, lw, rb, rw, kw,
    )
    out = call(
        last_kernel,
        jax.ShapeDtypeStruct((SLOTS_C, BLK, BLK), jnp.float32),
        [SMEM_SPEC] * 2 + [VMEM_SPEC] * 3,
        VMEM_SPEC,
        [pltpu.VMEM(LEFT_PANEL, lb.dtype)],
        FLOPS,
        8 * SLOTS_C * BLK * BLK,
    )(lw2, kw, lb2, right, total)
    return out[None, None]


def solution(mesh):
    in_specs = (
        P("row", "col", None, None, None),
        P("row", "col", None),
        P("row", "col", None, None, None),
        P("row", "col", None),
        P("row", "col", None),
    )
    out_specs = P("row", "col", None, None, None)
    return jax.shard_map(
        on_device, mesh=mesh, in_specs=in_specs, out_specs=out_specs, check_vma=False
    )
```

```python
import jax
import jax.numpy as jnp
from jax import lax
from jax.experimental import pallas as pl
from jax.experimental.pallas import tpu as pltpu
from jax.sharding import PartitionSpec as P

BLK = 128
MB = 6
KW = 8
NB = 8
SLOTS_A = 24
SLOTS_B = 32
SLOTS_C = 24
STEP = 2
AXES = ("row", "col")
VMEM_LIMIT = 40 * 1024 * 1024

SMEM_SPEC = pl.BlockSpec(memory_space=pltpu.SMEM)
VMEM_SPEC = pl.BlockSpec(memory_space=pltpu.VMEM)
ANY_SPEC = pl.BlockSpec(memory_space=pl.ANY)


def plan_kernel(across, rw, rw2, kw, lw2, told, blocks, meta, packed, left_mask, keep_mask, sems):
    sends = across[0] == 0

    def right_at(s):
        return jnp.where(sends, rw[s], rw2[s])

    def keep_at(u):
        return jnp.where(sends, told[u], kw[u])

    def left_at(s):
        return jnp.where(sends, told[SLOTS_C + s], lw2[s])

    for k in range(KW + 1):
        left_mask[k] = 0
    for j in range(NB):
        keep_mask[j] = 0
    for s in range(SLOTS_A):
        w = left_at(s)
        bit = jnp.where(w < MB * KW, lax.shift_left(jnp.int32(1), w >> 3), 0)
        left_mask[w & 7] = left_mask[w & 7] | bit
    for u in range(SLOTS_C):
        w = keep_at(u)
        keep_mask[w & 7] = keep_mask[w & 7] | lax.shift_left(jnp.int32(1), w >> 3)

    def copy(s, n):
        return pltpu.make_async_copy(blocks.at[s], packed.at[n], sems.at[n])

    n = jnp.int32(0)
    for s in range(SLOTS_B):
        w = right_at(s)
        need = (left_mask[w >> 3] & keep_mask[w & 7]) != 0

        @pl.when(need)
        def _(s=s, n=n, w=w):
            meta[1 + n] = w

            @pl.when(sends)
            def _():
                copy(s, n).start()

        n = n + need.astype(jnp.int32)
    meta[0] = n

    @pl.when(sends)
    def _():
        @pl.loop(0, n)
        def _(t):
            copy(0, t).wait()


def fill_right(panel, where_at, blocks, count):
    @pl.loop(0, count)
    def _(s):
        w = where_at(s)
        at = pl.multiple_of((w >> 3) * BLK, BLK)
        panel[w & 7, pl.ds(at, BLK), :] = blocks[s]


def fill_left(panel, where, blocks):
    @pl.loop(0, MB + 1)
    def _(i):
        panel[i] = jnp.zeros(panel.shape[1:], panel.dtype)

    @pl.loop(0, SLOTS_A)
    def _(s):
        w = where[s]
        at = pl.multiple_of((w & 7) * BLK, BLK)
        panel[w >> 3, :, pl.ds(at, BLK)] = blocks[s]


def clear_right(panel):
    @pl.loop(0, NB)
    def _(j):
        panel[j] = jnp.zeros(panel.shape[1:], panel.dtype)


def block_product(left, right, w):
    return jnp.dot(
        left[w >> 3], right[w & 7, : KW * BLK, :], preferred_element_type=jnp.float32
    )


def own_kernel(lw, rw, kw, left_blocks, right_blocks, total, left, right):
    fill_left(left, lw, left_blocks)
    clear_right(right)
    fill_right(right, lambda s: rw[s], right_blocks, SLOTS_B)

    @pl.loop(0, SLOTS_C)
    def _(u):
        total[u] = block_product(left, right, kw[u])


def right_kernel(across, meta, rw, arrived, beside, right):
    clear_right(right)

    @pl.when(across[0] == 0)
    def _():
        fill_right(right, lambda s: rw[s], beside, SLOTS_B)

    @pl.when(across[0] != 0)
    def _():
        fill_right(right, lambda s: meta[1 + s], arrived, meta[0])


def last_kernel(lw, kw, left_blocks, right, total, out, left):
    fill_left(left, lw, left_blocks)
    for u in range(SLOTS_C):
        out[u] = total[u] + block_product(left, right, kw[u])


def call(kernel, out_shape, in_specs, out_specs, scratch, flops, moved):
    return pl.pallas_call(
        kernel,
        out_shape=out_shape,
        in_specs=in_specs,
        out_specs=out_specs,
        scratch_shapes=scratch,
        compiler_params=pltpu.CompilerParams(vmem_limit_bytes=VMEM_LIMIT),
        cost_estimate=pl.CostEstimate(flops=flops, bytes_accessed=moved, transcendentals=0),
    )


LEFT_PANEL = (MB + 1, BLK, KW * BLK)
RIGHT_PANEL = (NB, (KW + 1) * BLK, BLK)
FLOPS = 2 * SLOTS_C * KW * BLK**3


def on_device(left_blocks, left_where, right_blocks, right_where, keep_where):
    lb, lw = left_blocks[0, 0], left_where[0, 0]
    rb, rw = right_blocks[0, 0], right_where[0, 0]
    kw = keep_where[0, 0]
    rows, cols = lax.axis_size("row"), lax.axis_size("col")

    def at(p, q):
        return (p % rows) * cols + q % cols

    grid = [(p, q) for p in range(rows) for q in range(cols)]
    across = [(at(p + 1, q), at(p, q)) for p, q in grid if p % 2 == 1]
    beside = [(at(p + 1, q), at(p, q)) for p, q in grid if p % 2 == 0]
    back = [(b, a) for a, b in across]
    left_on = [(at(p, q + 1), at(p, q)) for p, q in grid]
    side = (lax.axis_index("row") % 2).astype(jnp.int32)[None]

    lw2 = lax.ppermute(lw, AXES, left_on)
    rw2 = lax.ppermute(rw, AXES, across + beside)
    told = lax.ppermute(jnp.concatenate([kw, lw2]), AXES, back)
    lb_sent, _ = lax.optimization_barrier((lb, (lw2, rw2)))
    lb2 = lax.ppermute(lb_sent, AXES, left_on)
    beside_blocks = lax.ppermute(rb, AXES, beside)

    meta, packed = call(
        plan_kernel,
        (
            jax.ShapeDtypeStruct((SLOTS_B + 1,), jnp.int32),
            jax.ShapeDtypeStruct(rb.shape, rb.dtype),
        ),
        [SMEM_SPEC] * 6 + [ANY_SPEC],
        (SMEM_SPEC, VMEM_SPEC),
        [
            pltpu.SMEM((KW + 1,), jnp.int32),
            pltpu.SMEM((NB,), jnp.int32),
            pltpu.SemaphoreType.DMA((SLOTS_B,)),
        ],
        0,
        2 * rb.size,
    )(side, rw, rw2, kw, lw2, told, rb)

    def branch(size):
        def body(packed, meta, rw2, beside_blocks, lb, lw, rb, rw, kw):
            arrived = lax.ppermute(packed[:size], AXES, across)
            total = call(
                own_kernel,
                jax.ShapeDtypeStruct((SLOTS_C, BLK, BLK), jnp.float32),
                [SMEM_SPEC] * 3 + [VMEM_SPEC] * 2,
                VMEM_SPEC,
                [pltpu.VMEM(LEFT_PANEL, lb.dtype), pltpu.VMEM(RIGHT_PANEL, rb.dtype)],
                FLOPS,
                4 * SLOTS_C * BLK * BLK,
            )(lw, rw, kw, lb, rb)
            right = call(
                right_kernel,
                jax.ShapeDtypeStruct(RIGHT_PANEL, rb.dtype),
                [SMEM_SPEC] * 3 + [VMEM_SPEC] * 2,
                VMEM_SPEC,
                [],
                0,
                2 * rb.size,
            )(side, meta, rw2, arrived, beside_blocks)
            return total, right

        return body

    sizes = range(STEP, SLOTS_B + 1, STEP)
    pick = jnp.maximum((meta[0] + (STEP - 1)) // STEP, 1) - 1
    total, right = lax.switch(
        pick,
        [branch(size) for size in sizes],
        packed, meta, rw2, beside_blocks, lb, lw, rb, rw, kw,
    )
    out = call(
        last_kernel,
        jax.ShapeDtypeStruct((SLOTS_C, BLK, BLK), jnp.float32),
        [SMEM_SPEC] * 2 + [VMEM_SPEC] * 3,
        VMEM_SPEC,
        [pltpu.VMEM(LEFT_PANEL, lb.dtype)],
        FLOPS,
        8 * SLOTS_C * BLK * BLK,
    )(lw2, kw, lb2, right, total)
    return out[None, None]


def solution(mesh):
    in_specs = (
        P("row", "col", None, None, None),
        P("row", "col", None),
        P("row", "col", None, None, None),
        P("row", "col", None),
        P("row", "col", None),
    )
    out_specs = P("row", "col", None, None, None)
    return jax.shard_map(
        on_device, mesh=mesh, in_specs=in_specs, out_specs=out_specs, check_vma=False
    )
```

```python
import jax
import jax.numpy as jnp
from jax import lax
from jax.experimental import pallas as pl
from jax.experimental.pallas import tpu as pltpu
from jax.sharding import PartitionSpec as P

BLK = 128
MB = 6
KW = 8
NB = 8
SLOTS_A = 24
SLOTS_B = 32
SLOTS_C = 24
STEP = 1
AXES = ("row", "col")
VMEM_LIMIT = 40 * 1024 * 1024

SMEM_SPEC = pl.BlockSpec(memory_space=pltpu.SMEM)
VMEM_SPEC = pl.BlockSpec(memory_space=pltpu.VMEM)
ANY_SPEC = pl.BlockSpec(memory_space=pl.ANY)


def plan_kernel(across, rw, rw2, kw, lw2, told, blocks, meta, packed, left_mask, keep_mask, sems):
    sends = across[0] == 0

    def right_at(s):
        return jnp.where(sends, rw[s], rw2[s])

    def keep_at(u):
        return jnp.where(sends, told[u], kw[u])

    def left_at(s):
        return jnp.where(sends, told[SLOTS_C + s], lw2[s])

    for k in range(KW + 1):
        left_mask[k] = 0
    for j in range(NB):
        keep_mask[j] = 0
    for s in range(SLOTS_A):
        w = left_at(s)
        bit = jnp.where(w < MB * KW, lax.shift_left(jnp.int32(1), w >> 3), 0)
        left_mask[w & 7] = left_mask[w & 7] | bit
    for u in range(SLOTS_C):
        w = keep_at(u)
        keep_mask[w & 7] = keep_mask[w & 7] | lax.shift_left(jnp.int32(1), w >> 3)

    def copy(s, n):
        return pltpu.make_async_copy(blocks.at[s], packed.at[n], sems.at[n])

    n = jnp.int32(0)
    for s in range(SLOTS_B):
        w = right_at(s)
        need = (left_mask[w >> 3] & keep_mask[w & 7]) != 0

        @pl.when(need)
        def _(s=s, n=n, w=w):
            meta[1 + n] = w

            @pl.when(sends)
            def _():
                copy(s, n).start()

        n = n + need.astype(jnp.int32)
    meta[0] = n

    @pl.when(sends)
    def _():
        @pl.loop(0, n)
        def _(t):
            copy(0, t).wait()


def fill_right(panel, where_at, blocks, count):
    @pl.loop(0, count)
    def _(s):
        w = where_at(s)
        at = pl.multiple_of((w >> 3) * BLK, BLK)
        panel[w & 7, pl.ds(at, BLK), :] = blocks[s]


def fill_left(panel, where, blocks):
    @pl.loop(0, MB + 1)
    def _(i):
        panel[i] = jnp.zeros(panel.shape[1:], panel.dtype)

    @pl.loop(0, SLOTS_A)
    def _(s):
        w = where[s]
        at = pl.multiple_of((w & 7) * BLK, BLK)
        panel[w >> 3, :, pl.ds(at, BLK)] = blocks[s]


def clear_right(panel):
    @pl.loop(0, NB)
    def _(j):
        panel[j] = jnp.zeros(panel.shape[1:], panel.dtype)


def block_product(left, right, w):
    return jnp.dot(
        left[w >> 3], right[w & 7, : KW * BLK, :], preferred_element_type=jnp.float32
    )


def own_kernel(lw, rw, kw, left_blocks, right_blocks, total, left, right):
    fill_left(left, lw, left_blocks)
    clear_right(right)
    fill_right(right, lambda s: rw[s], right_blocks, SLOTS_B)

    @pl.loop(0, SLOTS_C)
    def _(u):
        total[u] = block_product(left, right, kw[u])


def right_kernel(across, meta, rw, arrived, beside, right):
    clear_right(right)

    @pl.when(across[0] == 0)
    def _():
        fill_right(right, lambda s: rw[s], beside, SLOTS_B)

    @pl.when(across[0] != 0)
    def _():
        fill_right(right, lambda s: meta[1 + s], arrived, meta[0])


def last_kernel(lw, kw, left_blocks, right, total, out, left):
    fill_left(left, lw, left_blocks)
    for u in range(SLOTS_C):
        out[u] = total[u] + block_product(left, right, kw[u])


def call(kernel, out_shape, in_specs, out_specs, scratch, flops, moved):
    return pl.pallas_call(
        kernel,
        out_shape=out_shape,
        in_specs=in_specs,
        out_specs=out_specs,
        scratch_shapes=scratch,
        compiler_params=pltpu.CompilerParams(vmem_limit_bytes=VMEM_LIMIT),
        cost_estimate=pl.CostEstimate(flops=flops, bytes_accessed=moved, transcendentals=0),
    )


LEFT_PANEL = (MB + 1, BLK, KW * BLK)
RIGHT_PANEL = (NB, (KW + 1) * BLK, BLK)
FLOPS = 2 * SLOTS_C * KW * BLK**3


def on_device(left_blocks, left_where, right_blocks, right_where, keep_where):
    lb, lw = left_blocks[0, 0], left_where[0, 0]
    rb, rw = right_blocks[0, 0], right_where[0, 0]
    kw = keep_where[0, 0]
    rows, cols = lax.axis_size("row"), lax.axis_size("col")

    def at(p, q):
        return (p % rows) * cols + q % cols

    grid = [(p, q) for p in range(rows) for q in range(cols)]
    across = [(at(p + 1, q), at(p, q)) for p, q in grid if p % 2 == 1]
    beside = [(at(p + 1, q), at(p, q)) for p, q in grid if p % 2 == 0]
    back = [(b, a) for a, b in across]
    left_on = [(at(p, q + 1), at(p, q)) for p, q in grid]
    side = (lax.axis_index("row") % 2).astype(jnp.int32)[None]

    lw2 = lax.ppermute(lw, AXES, left_on)
    rw2 = lax.ppermute(rw, AXES, across + beside)
    told = lax.ppermute(jnp.concatenate([kw, lw2]), AXES, back)
    lb_sent, _ = lax.optimization_barrier((lb, (lw2, rw2)))
    lb2 = lax.ppermute(lb_sent, AXES, left_on)
    beside_blocks = lax.ppermute(rb, AXES, beside)

    meta, packed = call(
        plan_kernel,
        (
            jax.ShapeDtypeStruct((SLOTS_B + 1,), jnp.int32),
            jax.ShapeDtypeStruct(rb.shape, rb.dtype),
        ),
        [SMEM_SPEC] * 6 + [ANY_SPEC],
        (SMEM_SPEC, VMEM_SPEC),
        [
            pltpu.SMEM((KW + 1,), jnp.int32),
            pltpu.SMEM((NB,), jnp.int32),
            pltpu.SemaphoreType.DMA((SLOTS_B,)),
        ],
        0,
        2 * rb.size,
    )(side, rw, rw2, kw, lw2, told, rb)

    def branch(size):
        def body(packed, meta, rw2, beside_blocks, lb, lw, rb, rw, kw):
            arrived = lax.ppermute(packed[:size], AXES, across)
            total = call(
                own_kernel,
                jax.ShapeDtypeStruct((SLOTS_C, BLK, BLK), jnp.float32),
                [SMEM_SPEC] * 3 + [VMEM_SPEC] * 2,
                VMEM_SPEC,
                [pltpu.VMEM(LEFT_PANEL, lb.dtype), pltpu.VMEM(RIGHT_PANEL, rb.dtype)],
                FLOPS,
                4 * SLOTS_C * BLK * BLK,
            )(lw, rw, kw, lb, rb)
            right = call(
                right_kernel,
                jax.ShapeDtypeStruct(RIGHT_PANEL, rb.dtype),
                [SMEM_SPEC] * 3 + [VMEM_SPEC] * 2,
                VMEM_SPEC,
                [],
                0,
                2 * rb.size,
            )(side, meta, rw2, arrived, beside_blocks)
            return total, right

        return body

    sizes = range(STEP, SLOTS_B + 1, STEP)
    pick = jnp.maximum((meta[0] + (STEP - 1)) // STEP, 1) - 1
    total, right = lax.switch(
        pick,
        [branch(size) for size in sizes],
        packed, meta, rw2, beside_blocks, lb, lw, rb, rw, kw,
    )
    out = call(
        last_kernel,
        jax.ShapeDtypeStruct((SLOTS_C, BLK, BLK), jnp.float32),
        [SMEM_SPEC] * 2 + [VMEM_SPEC] * 3,
        VMEM_SPEC,
        [pltpu.VMEM(LEFT_PANEL, lb.dtype)],
        FLOPS,
        8 * SLOTS_C * BLK * BLK,
    )(lw2, kw, lb2, right, total)
    return out[None, None]


def solution(mesh):
    in_specs = (
        P("row", "col", None, None, None),
        P("row", "col", None),
        P("row", "col", None, None, None),
        P("row", "col", None),
        P("row", "col", None),
    )
    out_specs = P("row", "col", None, None, None)
    return jax.shard_map(
        on_device, mesh=mesh, in_specs=in_specs, out_specs=out_specs, check_vma=False
    )
```

```python
import jax
import jax.numpy as jnp
from jax import lax
from jax.experimental import pallas as pl
from jax.experimental.pallas import tpu as pltpu
from jax.sharding import PartitionSpec as P

BLK = 128
MB = 6
KW = 8
NB = 8
SLOTS_A = 24
SLOTS_B = 32
SLOTS_C = 24
STEP = 1
AXES = ("row", "col")
VMEM_LIMIT = 40 * 1024 * 1024

SMEM_SPEC = pl.BlockSpec(memory_space=pltpu.SMEM)
VMEM_SPEC = pl.BlockSpec(memory_space=pltpu.VMEM)
ANY_SPEC = pl.BlockSpec(memory_space=pl.ANY)


def plan_kernel(across, rw, rw2, kw, lw2, told, blocks, meta, packed, left_mask, keep_mask, sems):
    sends = across[0] == 0

    def right_at(s):
        return jnp.where(sends, rw[s], rw2[s])

    def keep_at(u):
        return jnp.where(sends, told[u], kw[u])

    def left_at(s):
        return jnp.where(sends, told[SLOTS_C + s], lw2[s])

    for k in range(KW + 1):
        left_mask[k] = 0
    for j in range(NB):
        keep_mask[j] = 0
    for s in range(SLOTS_A):
        w = left_at(s)
        bit = jnp.where(w < MB * KW, lax.shift_left(jnp.int32(1), w >> 3), 0)
        left_mask[w & 7] = left_mask[w & 7] | bit
    for u in range(SLOTS_C):
        w = keep_at(u)
        keep_mask[w & 7] = keep_mask[w & 7] | lax.shift_left(jnp.int32(1), w >> 3)

    def copy(s, n):
        return pltpu.make_async_copy(blocks.at[s], packed.at[n], sems.at[n])

    n = jnp.int32(0)
    for s in range(SLOTS_B):
        w = right_at(s)
        need = (left_mask[w >> 3] & keep_mask[w & 7]) != 0

        @pl.when(need)
        def _(s=s, n=n, w=w):
            meta[1 + n] = w

            @pl.when(sends)
            def _():
                copy(s, n).start()

        n = n + need.astype(jnp.int32)
    meta[0] = n

    @pl.when(sends)
    def _():
        @pl.loop(0, n)
        def _(t):
            copy(0, t).wait()


def fill_right(panel, where_at, blocks, count):
    @pl.loop(0, count)
    def _(s):
        w = where_at(s)
        at = pl.multiple_of((w >> 3) * BLK, BLK)
        panel[w & 7, pl.ds(at, BLK), :] = blocks[s]


def fill_left(panel, where, blocks):
    @pl.loop(0, MB + 1)
    def _(i):
        panel[i] = jnp.zeros(panel.shape[1:], panel.dtype)

    @pl.loop(0, SLOTS_A)
    def _(s):
        w = where[s]
        at = pl.multiple_of((w & 7) * BLK, BLK)
        panel[w >> 3, :, pl.ds(at, BLK)] = blocks[s]


def clear_right(panel):
    @pl.loop(0, NB)
    def _(j):
        panel[j] = jnp.zeros(panel.shape[1:], panel.dtype)


def block_product(left, right, w):
    return jnp.dot(
        left[w >> 3], right[w & 7, : KW * BLK, :], preferred_element_type=jnp.float32
    )


def own_kernel(lw, rw, kw, left_blocks, right_blocks, total, left, right):
    fill_left(left, lw, left_blocks)
    clear_right(right)
    fill_right(right, lambda s: rw[s], right_blocks, SLOTS_B)

    @pl.loop(0, SLOTS_C)
    def _(u):
        total[u] = block_product(left, right, kw[u])


def right_kernel(across, meta, rw, arrived, beside, right):
    clear_right(right)

    @pl.when(across[0] == 0)
    def _():
        fill_right(right, lambda s: rw[s], beside, SLOTS_B)

    @pl.when(across[0] != 0)
    def _():
        fill_right(right, lambda s: meta[1 + s], arrived, meta[0])


def last_kernel(lw, kw, left_blocks, right, total, out, left, ready, sems):
    fill_left(left, lw, left_blocks)

    def copy(u):
        return pltpu.make_async_copy(ready.at[u], out.at[u], sems.at[u])

    for u in range(SLOTS_C):
        ready[u] = total[u] + block_product(left, right, kw[u])
        copy(u).start()
    for u in range(SLOTS_C):
        copy(u).wait()


def call(kernel, out_shape, in_specs, out_specs, scratch, flops, moved):
    return pl.pallas_call(
        kernel,
        out_shape=out_shape,
        in_specs=in_specs,
        out_specs=out_specs,
        scratch_shapes=scratch,
        compiler_params=pltpu.CompilerParams(vmem_limit_bytes=VMEM_LIMIT),
        cost_estimate=pl.CostEstimate(flops=flops, bytes_accessed=moved, transcendentals=0),
    )


LEFT_PANEL = (MB + 1, BLK, KW * BLK)
RIGHT_PANEL = (NB, (KW + 1) * BLK, BLK)
FLOPS = 2 * SLOTS_C * KW * BLK**3


def on_device(left_blocks, left_where, right_blocks, right_where, keep_where):
    lb, lw = left_blocks[0, 0], left_where[0, 0]
    rb, rw = right_blocks[0, 0], right_where[0, 0]
    kw = keep_where[0, 0]
    rows, cols = lax.axis_size("row"), lax.axis_size("col")

    def at(p, q):
        return (p % rows) * cols + q % cols

    grid = [(p, q) for p in range(rows) for q in range(cols)]
    across = [(at(p + 1, q), at(p, q)) for p, q in grid if p % 2 == 1]
    beside = [(at(p + 1, q), at(p, q)) for p, q in grid if p % 2 == 0]
    back = [(b, a) for a, b in across]
    left_on = [(at(p, q + 1), at(p, q)) for p, q in grid]
    side = (lax.axis_index("row") % 2).astype(jnp.int32)[None]

    lw2 = lax.ppermute(lw, AXES, left_on)
    rw2 = lax.ppermute(rw, AXES, across + beside)
    note = jnp.concatenate([kw, lw2])
    note, rw2 = lax.optimization_barrier((note, rw2))
    told = lax.ppermute(note, AXES, back)
    lb_sent, _ = lax.optimization_barrier((lb, (lw2, rw2)))
    lb2 = lax.ppermute(lb_sent, AXES, left_on)
    rb_sent, _ = lax.optimization_barrier((rb, note))
    beside_blocks = lax.ppermute(rb_sent, AXES, beside)

    meta, packed = call(
        plan_kernel,
        (
            jax.ShapeDtypeStruct((SLOTS_B + 1,), jnp.int32),
            jax.ShapeDtypeStruct(rb.shape, rb.dtype),
        ),
        [SMEM_SPEC] * 6 + [ANY_SPEC],
        (SMEM_SPEC, VMEM_SPEC),
        [
            pltpu.SMEM((KW + 1,), jnp.int32),
            pltpu.SMEM((NB,), jnp.int32),
            pltpu.SemaphoreType.DMA((SLOTS_B,)),
        ],
        0,
        2 * rb.size,
    )(side, rw, rw2, kw, lw2, told, rb)

    def branch(size):
        def body(packed, meta, rw2, beside_blocks, lb, lw, rb, rw, kw):
            arrived = lax.ppermute(packed[:size], AXES, across)
            total = call(
                own_kernel,
                jax.ShapeDtypeStruct((SLOTS_C, BLK, BLK), jnp.float32),
                [SMEM_SPEC] * 3 + [VMEM_SPEC] * 2,
                VMEM_SPEC,
                [pltpu.VMEM(LEFT_PANEL, lb.dtype), pltpu.VMEM(RIGHT_PANEL, rb.dtype)],
                FLOPS,
                4 * SLOTS_C * BLK * BLK,
            )(lw, rw, kw, lb, rb)
            right = call(
                right_kernel,
                jax.ShapeDtypeStruct(RIGHT_PANEL, rb.dtype),
                [SMEM_SPEC] * 3 + [VMEM_SPEC] * 2,
                VMEM_SPEC,
                [],
                0,
                2 * rb.size,
            )(side, meta, rw2, arrived, beside_blocks)
            return total, right

        return body

    sizes = range(STEP, SLOTS_B + 1, STEP)
    pick = jnp.maximum((meta[0] + (STEP - 1)) // STEP, 1) - 1
    total, right = lax.switch(
        pick,
        [branch(size) for size in sizes],
        packed, meta, rw2, beside_blocks, lb, lw, rb, rw, kw,
    )
    out = call(
        last_kernel,
        jax.ShapeDtypeStruct((SLOTS_C, BLK, BLK), jnp.float32),
        [SMEM_SPEC] * 2 + [VMEM_SPEC] * 3,
        ANY_SPEC,
        [
            pltpu.VMEM(LEFT_PANEL, lb.dtype),
            pltpu.VMEM((SLOTS_C, BLK, BLK), jnp.float32),
            pltpu.SemaphoreType.DMA((SLOTS_C,)),
        ],
        FLOPS,
        8 * SLOTS_C * BLK * BLK,
    )(lw2, kw, lb2, right, total)
    return out[None, None]


def solution(mesh):
    in_specs = (
        P("row", "col", None, None, None),
        P("row", "col", None),
        P("row", "col", None, None, None),
        P("row", "col", None),
        P("row", "col", None),
    )
    out_specs = P("row", "col", None, None, None)
    return jax.shard_map(
        on_device, mesh=mesh, in_specs=in_specs, out_specs=out_specs, check_vma=False
    )
```

```python
import jax
import jax.numpy as jnp
from jax import lax
from jax.experimental import pallas as pl
from jax.experimental.pallas import tpu as pltpu
from jax.sharding import PartitionSpec as P

BLK = 128
MB = 6
KW = 8
NB = 8
SLOTS_A = 24
SLOTS_B = 32
SLOTS_C = 24
STEP = 1
RUN = 8
AXES = ("row", "col")
VMEM_LIMIT = 40 * 1024 * 1024

SMEM_SPEC = pl.BlockSpec(memory_space=pltpu.SMEM)
VMEM_SPEC = pl.BlockSpec(memory_space=pltpu.VMEM)
ANY_SPEC = pl.BlockSpec(memory_space=pl.ANY)


def plan_kernel(across, rw, rw2, kw, lw2, told, blocks, meta, packed, left_mask, keep_mask, sems):
    sends = across[0] == 0

    def right_at(s):
        return jnp.where(sends, rw[s], rw2[s])

    def keep_at(u):
        return jnp.where(sends, told[u], kw[u])

    def left_at(s):
        return jnp.where(sends, told[SLOTS_C + s], lw2[s])

    for k in range(KW + 1):
        left_mask[k] = 0
    for j in range(NB):
        keep_mask[j] = 0
    for s in range(SLOTS_A):
        w = left_at(s)
        bit = jnp.where(w < MB * KW, lax.shift_left(jnp.int32(1), w >> 3), 0)
        left_mask[w & 7] = left_mask[w & 7] | bit
    for u in range(SLOTS_C):
        w = keep_at(u)
        keep_mask[w & 7] = keep_mask[w & 7] | lax.shift_left(jnp.int32(1), w >> 3)

    def copy(s, n):
        return pltpu.make_async_copy(blocks.at[s], packed.at[n], sems.at[n])

    n = jnp.int32(0)
    for s in range(SLOTS_B):
        w = right_at(s)
        need = (left_mask[w >> 3] & keep_mask[w & 7]) != 0

        @pl.when(need)
        def _(s=s, n=n, w=w):
            meta[1 + n] = w

            @pl.when(sends)
            def _():
                copy(s, n).start()

        n = n + need.astype(jnp.int32)
    meta[0] = n

    @pl.when(sends)
    def _():
        @pl.loop(0, n)
        def _(t):
            copy(0, t).wait()


def fill_right(panel, where_at, blocks, count):
    @pl.loop(0, count)
    def _(s):
        w = where_at(s)
        at = pl.multiple_of((w >> 3) * BLK, BLK)
        panel[w & 7, pl.ds(at, BLK), :] = blocks[s]


def fill_left(panel, where, blocks):
    @pl.loop(0, MB + 1)
    def _(i):
        panel[i] = jnp.zeros(panel.shape[1:], panel.dtype)

    @pl.loop(0, SLOTS_A)
    def _(s):
        w = where[s]
        at = pl.multiple_of((w & 7) * BLK, BLK)
        panel[w >> 3, :, pl.ds(at, BLK)] = blocks[s]


def clear_right(panel):
    @pl.loop(0, NB)
    def _(j):
        panel[j] = jnp.zeros(panel.shape[1:], panel.dtype)


def block_product(left, right, w):
    return jnp.dot(
        left[w >> 3], right[w & 7, : KW * BLK, :], preferred_element_type=jnp.float32
    )


def own_kernel(lw, rw, kw, left_blocks, right_blocks, total, left, right):
    fill_left(left, lw, left_blocks)
    clear_right(right)
    fill_right(right, lambda s: rw[s], right_blocks, SLOTS_B)

    @pl.loop(0, SLOTS_C)
    def _(u):
        total[u] = block_product(left, right, kw[u])


def right_kernel(across, meta, rw, arrived, beside, right):
    clear_right(right)

    @pl.when(across[0] == 0)
    def _():
        fill_right(right, lambda s: rw[s], beside, SLOTS_B)

    @pl.when(across[0] != 0)
    def _():
        fill_right(right, lambda s: meta[1 + s], arrived, meta[0])


def last_kernel(
    soon, lw, kw, soon_blocks, late_blocks, right, total, out, left, ready, sems
):
    @pl.when(soon[0] != 0)
    def _():
        fill_left(left, lw, soon_blocks)

    @pl.when(soon[0] == 0)
    def _():
        fill_left(left, lw, late_blocks)

    def copy(u):
        return pltpu.make_async_copy(ready.at[u], out.at[u], sems.at[u])

    for u in range(SLOTS_C):
        ready[u] = total[u] + block_product(left, right, kw[u])
        copy(u).start()
    for u in range(SLOTS_C):
        copy(u).wait()


def call(kernel, out_shape, in_specs, out_specs, scratch, flops, moved):
    return pl.pallas_call(
        kernel,
        out_shape=out_shape,
        in_specs=in_specs,
        out_specs=out_specs,
        scratch_shapes=scratch,
        compiler_params=pltpu.CompilerParams(vmem_limit_bytes=VMEM_LIMIT),
        cost_estimate=pl.CostEstimate(flops=flops, bytes_accessed=moved, transcendentals=0),
    )


LEFT_PANEL = (MB + 1, BLK, KW * BLK)
RIGHT_PANEL = (NB, (KW + 1) * BLK, BLK)
FLOPS = 2 * SLOTS_C * KW * BLK**3


def on_device(left_blocks, left_where, right_blocks, right_where, keep_where):
    lb, lw = left_blocks[0, 0], left_where[0, 0]
    rb, rw = right_blocks[0, 0], right_where[0, 0]
    kw = keep_where[0, 0]
    rows, cols = lax.axis_size("row"), lax.axis_size("col")

    def at(p, q):
        return (p % rows) * cols + q % cols

    grid = [(p, q) for p in range(rows) for q in range(cols)]
    across = [(at(p + 1, q), at(p, q)) for p, q in grid if p % 2 == 1]
    beside = [(at(p + 1, q), at(p, q)) for p, q in grid if p % 2 == 0]
    back = [(b, a) for a, b in across]
    left_on = [(at(p, q + 1), at(p, q)) for p, q in grid]
    left_soon = [(at(p, q + 1), at(p, q)) for p, q in grid if (q + 1) % RUN]
    left_late = [(at(p, q + 1), at(p, q)) for p, q in grid if (q + 1) % RUN == 0]
    soon = (lax.axis_index("col") % RUN != RUN - 1).astype(jnp.int32)[None]
    side = (lax.axis_index("row") % 2).astype(jnp.int32)[None]

    lw2 = lax.ppermute(lw, AXES, left_on)
    rw2 = lax.ppermute(rw, AXES, across + beside)
    told = lax.ppermute(jnp.concatenate([kw, lw2]), AXES, back)
    lb_soon = lax.ppermute(lb, AXES, left_soon)
    lb_sent, _ = lax.optimization_barrier((lb, (lw2, rw2)))
    lb_late = lax.ppermute(lb_sent, AXES, left_late)
    beside_blocks = lax.ppermute(rb, AXES, beside)

    meta, packed = call(
        plan_kernel,
        (
            jax.ShapeDtypeStruct((SLOTS_B + 1,), jnp.int32),
            jax.ShapeDtypeStruct(rb.shape, rb.dtype),
        ),
        [SMEM_SPEC] * 6 + [ANY_SPEC],
        (SMEM_SPEC, VMEM_SPEC),
        [
            pltpu.SMEM((KW + 1,), jnp.int32),
            pltpu.SMEM((NB,), jnp.int32),
            pltpu.SemaphoreType.DMA((SLOTS_B,)),
        ],
        0,
        2 * rb.size,
    )(side, rw, rw2, kw, lw2, told, rb)

    def branch(size):
        def body(packed, meta, rw2, beside_blocks, lb, lw, rb, rw, kw):
            arrived = lax.ppermute(packed[:size], AXES, across)
            total = call(
                own_kernel,
                jax.ShapeDtypeStruct((SLOTS_C, BLK, BLK), jnp.float32),
                [SMEM_SPEC] * 3 + [VMEM_SPEC] * 2,
                VMEM_SPEC,
                [pltpu.VMEM(LEFT_PANEL, lb.dtype), pltpu.VMEM(RIGHT_PANEL, rb.dtype)],
                FLOPS,
                4 * SLOTS_C * BLK * BLK,
            )(lw, rw, kw, lb, rb)
            right = call(
                right_kernel,
                jax.ShapeDtypeStruct(RIGHT_PANEL, rb.dtype),
                [SMEM_SPEC] * 3 + [VMEM_SPEC] * 2,
                VMEM_SPEC,
                [],
                0,
                2 * rb.size,
            )(side, meta, rw2, arrived, beside_blocks)
            return total, right

        return body

    sizes = range(STEP, SLOTS_B + 1, STEP)
    pick = jnp.maximum((meta[0] + (STEP - 1)) // STEP, 1) - 1
    total, right = lax.switch(
        pick,
        [branch(size) for size in sizes],
        packed, meta, rw2, beside_blocks, lb, lw, rb, rw, kw,
    )
    out = call(
        last_kernel,
        jax.ShapeDtypeStruct((SLOTS_C, BLK, BLK), jnp.float32),
        [SMEM_SPEC] * 3 + [VMEM_SPEC] * 4,
        ANY_SPEC,
        [
            pltpu.VMEM(LEFT_PANEL, lb.dtype),
            pltpu.VMEM((SLOTS_C, BLK, BLK), jnp.float32),
            pltpu.SemaphoreType.DMA((SLOTS_C,)),
        ],
        FLOPS,
        8 * SLOTS_C * BLK * BLK,
    )(soon, lw2, kw, lb_soon, lb_late, right, total)
    return out[None, None]


def solution(mesh):
    in_specs = (
        P("row", "col", None, None, None),
        P("row", "col", None),
        P("row", "col", None, None, None),
        P("row", "col", None),
        P("row", "col", None),
    )
    out_specs = P("row", "col", None, None, None)
    return jax.shard_map(
        on_device, mesh=mesh, in_specs=in_specs, out_specs=out_specs, check_vma=False
    )
```
